512 devices in a mesh: leaf: 16 (over z), row: 8 (over y, core), col: 4 (over x).
Axes of the slice: x: 4, y: 4, z: 16, core: 2. Of those that a mesh axis runs over, the one named last changes fastest.
Arguments:
- right_root: float32 [8, 4096], P(None, ('leaf', 'row')), may hold values from -6 to 6
- right_middle: float32 [8, 8192], P(None, ('leaf', 'row')), may hold values from -6 to 6
- right_lower: float32 [8, 16384], P(None, ('leaf', 'row')), may hold values from -6 to 6
- inverse_root: float32 [2, 4096, 4096], P(None, 'col', ('leaf', 'row')), may hold values from -0.09375 to 0.09375
- inverse_middle: float32 [2, 4096, 8192], P(None, 'col', ('leaf', 'row')), may hold values from -0.09375 to 0.09375
- inverse_lower: float32 [2, 4096, 16384], P(None, 'col', ('leaf', 'row')), may hold values from -0.09375 to 0.09375
- upward_middle: float32 [8192, 2048], P(('leaf', 'row'), 'col'), may hold values from -0.09375 to 0.09375
- upward_lower: float32 [16384, 2048], P(('leaf', 'row'), 'col'), may hold values from -0.09375 to 0.09375
- downward_middle: float32 [2048, 8192], P('col', ('leaf', 'row')), may hold values from -0.125 to 0.125
- downward_lower: float32 [2048, 16384], P('col', ('leaf', 'row')), may hold values from -0.125 to 0.125
- index_middle: int32 [2, 2048], P(None, 'col'), may hold values from 0 to 4095, as said below
- index_lower: int32 [4, 2048], P(None, 'col'), may hold values from 0 to 4095, as said below
Outputs:
- solution_root: float32 [8, 4096], P(None, ('leaf', 'row'))
- solution_middle: float32 [8, 8192], P(None, ('leaf', 'row'))
- solution_lower: float32 [8, 16384], P(None, ('leaf', 'row'))
The draws below stay inside these ranges and needn't reach their ends.
Inputs may be any that keep to these rules, and one draw needn't show every extreme that they name: `index_middle`: row f lists 2048 distinct positions in the separator of the parent of middle front f; the two rows may share positions. `index_lower`: row f lists 2048 distinct positions in the separator of middle front f // 2; sibling rows may share positions.
All inputs are finite; a program needn't handle non-finite values.
Results may differ from the reference program's by a relative error of at most 0.00019.
Values sent between devices are 32-bit elements; how exact they have to be, the bound alone decides.
No kernel may reach another device: no remote copies, remote signals or barrier semaphores. Data moves between devices by JAX's collectives and lax.ppermute only.
A program may use at most 64 MiB of HBM per device.

```python
import jax
import jax.numpy as jnp
from jax import lax

S = 4096
UPD = 2048
NRHS = 8


def draw_positions(key, row_total):
    row_keys = jax.random.split(key, row_total)
    row_ids = jnp.arange(row_total, dtype=jnp.int32)

    def one_row(subkey, row_id):
        scores = jax.random.randint(subkey, (S,), 0, S, dtype=jnp.int32) * S + jnp.arange(S, dtype=jnp.int32)
        forced = scores.at[0].set(-2).at[S - 1].set(-1)
        scores = jnp.where(row_id == 0, forced, scores)
        return jnp.argsort(scores)[:UPD].astype(jnp.int32)
    return jax.vmap(one_row)(row_keys, row_ids)


def draw_index_middle(key, part):
    key = jax.random.fold_in(key, 11)
    return draw_positions(key, 2)


def draw_index_lower(key, part):
    key = jax.random.fold_in(key, 12)
    return draw_positions(key, 4)


def block_scale(rng, dims, cuts, least, high):
    level = 1.0
    for position, parts in cuts:
        steps = jax.random.uniform(jax.random.fold_in(jax.random.fold_in(rng, 6), position), (parts,), jnp.float32, least / len(cuts), high / len(cuts))
        level = level * jnp.repeat(jnp.exp(steps), dims[position] // parts).reshape((-1,) + (1,) * (len(dims) - 1 - position))
    return level


def noise(key, extent, width, reach, shards=(), held_as=jnp.bfloat16):
    values = width * jax.random.normal(key, extent, jnp.float32)
    if shards:
        values = values * block_scale(key, extent, shards, -0.22, 0.18)
    return jnp.clip(values, -reach, reach).astype(held_as)


def setup_inputs(seed: int = 0) -> dict:
    key_list = jax.random.split(jax.random.key(seed), 13)
    return {
        "right_root": noise(key_list[0], (NRHS, S), 1.0, 6.0, ((1, 128),), jnp.float32),
        "right_middle": noise(key_list[1], (NRHS, 2 * S), 1.0, 6.0, ((1, 128),), jnp.float32),
        "right_lower": noise(key_list[2], (NRHS, 4 * S), 1.0, 6.0, ((1, 128),), jnp.float32),
        "inverse_root": noise(key_list[3], (2, S, S), S ** -0.5, 0.09375, ((1, 4), (2, 128)), jnp.float32),
        "inverse_middle": noise(key_list[4], (2, S, 2 * S), S ** -0.5, 0.09375, ((1, 4), (2, 128)), jnp.float32),
        "inverse_lower": noise(key_list[5], (2, S, 4 * S), S ** -0.5, 0.09375, ((1, 4), (2, 128)), jnp.float32),
        "upward_middle": noise(key_list[6], (2 * S, UPD), S ** -0.5, 0.09375, ((0, 128), (1, 4)), jnp.float32),
        "upward_lower": noise(key_list[7], (4 * S, UPD), S ** -0.5, 0.09375, ((0, 128), (1, 4)), jnp.float32),
        "downward_middle": noise(key_list[8], (UPD, 2 * S), UPD ** -0.5, 0.125, ((0, 4), (1, 128)), jnp.float32),
        "downward_lower": noise(key_list[9], (UPD, 4 * S), UPD ** -0.5, 0.125, ((0, 4), (1, 128)), jnp.float32),
        "index_middle": draw_index_middle(jax.random.fold_in(key_list[12], 71), 0),
        "index_lower": draw_index_lower(jax.random.fold_in(key_list[12], 71), 0),
    }


def matmul_hi(left_side, right_side):
    return jnp.dot(left_side, right_side, precision=lax.Precision.HIGHEST, preferred_element_type=jnp.float32)


def columns(array, front_id):
    return array[..., front_id * S:(front_id + 1) * S]


def reference(right_root, right_middle, right_lower, inverse_root, inverse_middle, inverse_lower, upward_middle, upward_lower, downward_middle, downward_lower, index_middle, index_lower):
    rights = [right_root, right_middle, right_lower]
    inverses = [inverse_root, inverse_middle, inverse_lower]
    upwards = [None, upward_middle, upward_lower]
    downwards = [None, downward_middle, downward_lower]
    indices = [None, index_middle, index_lower]
    forward = [None, None, None]
    for level in (2, 1, 0):
        fronts = []
        for front_id in range(2 ** level):
            reduced = columns(rights[level], front_id)
            if level < 2:
                for child in (2 * front_id, 2 * front_id + 1):
                    update = matmul_hi(forward[level + 1][child], upwards[level + 1][child * S:(child + 1) * S, :])
                    placed = jnp.zeros((NRHS, S), jnp.float32).at[:, indices[level + 1][child]].add(update)
                    reduced = reduced - placed
            fronts.append(matmul_hi(reduced, columns(inverses[level][0], front_id)))
        forward[level] = fronts
    backward = [None, None, None]
    for level in (0, 1, 2):
        fronts = []
        for front_id in range(2 ** level):
            reduced = forward[level][front_id]
            if level > 0:
                parent = backward[level - 1][front_id // 2]
                picked = jnp.take(parent, indices[level][front_id], axis=1)
                reduced = reduced - matmul_hi(picked, columns(downwards[level], front_id))
            fronts.append(matmul_hi(reduced, columns(inverses[level][1], front_id)))
        backward[level] = fronts
    return (jnp.concatenate(backward[0], axis=1), jnp.concatenate(backward[1], axis=1), jnp.concatenate(backward[2], axis=1))
```

```python
import jax
import jax.numpy as jnp
from jax import lax
from jax.sharding import Mesh
from jax.sharding import PartitionSpec as P

S = 4096
QUARTER = 1024
SIZES = {"a": 2, "b": 2, "d": 4, "y": 4, "k": 2, "x": 4}


def count(axes):
    total = 1
    for axis in axes:
        total *= SIZES[axis]
    return total


def matmul_hi(left_side, right_side):
    return jnp.dot(
        left_side, right_side, precision=lax.Precision.HIGHEST, preferred_element_type=jnp.float32
    )


def exchange(pieces, axes):
    return lax.all_to_all(pieces, tuple(axes), 0, 0, tiled=False)


def gather(block, axes):
    return exchange(jnp.broadcast_to(block[None], (count(axes),) + block.shape), axes)


def total(block, axes):
    return jnp.sum(gather(block, axes), axis=0)


def flat(pieces):
    return pieces.transpose(1, 0, 2).reshape(pieces.shape[1], -1)


def quarter_of(pieces):
    x_at = lax.axis_index("x")
    parts = pieces.reshape((4, pieces.shape[0] // 4) + pieces.shape[1:])
    return flat(lax.dynamic_index_in_dim(parts, x_at, 0, keepdims=False))


def extend(product, positions, right_block, at, level_axes):
    first = (lax.axis_index("x") == 0).astype(jnp.float32)
    update = jnp.zeros((8, S), jnp.float32)
    update = lax.dynamic_update_slice_in_dim(update, right_block * first, at * right_block.shape[1], 1)
    update = update.at[:, positions].add(-product)
    pieces = update.reshape(8, 4, 8, 128).transpose(2, 1, 0, 3).reshape(32, 8, 128)
    own = jnp.sum(exchange(pieces, "ykx"), axis=0)
    own = total(own, level_axes)
    return flat(gather(own, "yk"))


def local(
    right_root,
    right_middle,
    right_lower,
    inverse_root,
    inverse_middle,
    inverse_lower,
    upward_middle,
    upward_lower,
    downward_middle,
    downward_lower,
    index_middle,
    index_lower,
):
    at = lax.axis_index
    front_middle = at("a")
    front_lower = at(("a", "b"))
    positions_middle = lax.dynamic_index_in_dim(index_middle, front_middle, 0, keepdims=False)
    positions_lower = lax.dynamic_index_in_dim(index_lower, front_lower, 0, keepdims=False)

    operand = quarter_of(gather(right_lower, "dyk"))
    z_lower = total(matmul_hi(operand, inverse_lower[0]), "x")
    w_middle = extend(
        matmul_hi(z_lower, upward_lower), positions_lower, right_middle, at(("b", "d", "y", "k")), "bd"
    )
    z_middle = total(matmul_hi(w_middle, inverse_middle[0]), "x")
    w_root = extend(
        matmul_hi(z_middle, upward_middle),
        positions_middle,
        right_root,
        at(("a", "b", "d", "y", "k")),
        "abd",
    )
    z_root = total(matmul_hi(w_root, inverse_root[0]), "x")
    operand = quarter_of(gather(z_root, "abdyk"))
    solution_root = total(matmul_hi(operand, inverse_root[1]), "x")
    whole = flat(gather(solution_root, "abdyk"))
    picked = jnp.take(whole, positions_middle, axis=1)
    v_middle = z_middle - total(matmul_hi(picked, downward_middle), "x")
    operand = quarter_of(gather(v_middle, "bdyk"))
    solution_middle = total(matmul_hi(operand, inverse_middle[1]), "x")
    whole = flat(gather(solution_middle, "bdyk"))
    picked = jnp.take(whole, positions_lower, axis=1)
    v_lower = z_lower - total(matmul_hi(picked, downward_lower), "x")
    operand = quarter_of(gather(v_lower, "dyk"))
    solution_lower = total(matmul_hi(operand, inverse_lower[1]), "x")
    return (solution_root, solution_middle, solution_lower)


def solution(mesh):
    split = Mesh(mesh.devices.reshape(tuple(SIZES.values())), tuple(SIZES))
    n = ("a", "b", "d", "y", "k")
    in_specs = (
        P(None, n),
        P(None, n),
        P(None, n),
        P(None, "x", n),
        P(None, "x", n),
        P(None, "x", n),
        P(n, "x"),
        P(n, "x"),
        P("x", n),
        P("x", n),
        P(None, "x"),
        P(None, "x"),
    )
    out_specs = (P(None, n), P(None, n), P(None, n))
    return jax.shard_map(local, mesh=split, in_specs=in_specs, out_specs=out_specs, check_vma=False)
```

```python
import functools

import jax
import jax.numpy as jnp
from jax import lax
from jax.experimental import pallas as pl
from jax.experimental.pallas import tpu as pltpu
from jax.sharding import Mesh
from jax.sharding import PartitionSpec as P

S = 4096
QUARTER = 1024
LANES = 128
SIZES = {"a": 2, "b": 2, "d": 4, "y": 4, "k": 2, "x": 4}
VMEM_LIMIT = 32 * 1024 * 1024


def count(axes):
    total = 1
    for axis in axes:
        total *= SIZES[axis]
    return total


def exchange(pieces, axes):
    return lax.all_to_all(pieces, tuple(axes), 0, 0, tiled=False)


def call(body, out_shapes, *operands, after=()):
    shapes = [jax.ShapeDtypeStruct(shape, jnp.float32) for shape in out_shapes]
    whole = pl.BlockSpec(memory_space=pltpu.VMEM)
    extra = len(after)
    return pl.pallas_call(
        lambda *refs: body(*refs[extra:]),
        out_shape=shapes[0] if len(shapes) == 1 else tuple(shapes),
        in_specs=[pl.BlockSpec(memory_space=pl.ANY)] * extra + [whole] * len(operands),
        out_specs=whole if len(shapes) == 1 else (whole,) * len(shapes),
        compiler_params=pltpu.CompilerParams(vmem_limit_bytes=VMEM_LIMIT),
    )(*after, *operands)


def product(left_side, right_side, transposed=False):
    def part(one, two):
        dims = (((1,), (1 if transposed else 0,)), ((), ()))
        return lax.dot_general(one, two, dims, preferred_element_type=jnp.float32)

    rows = left_side.shape[0]
    left_high = left_side.astype(jnp.bfloat16)
    left_low = (left_side - left_high.astype(jnp.float32)).astype(jnp.bfloat16)
    right_high = right_side.astype(jnp.bfloat16)
    right_low = (right_side - right_high.astype(jnp.float32)).astype(jnp.bfloat16)
    both = part(jnp.concatenate([left_high, left_low], axis=0), right_high)
    return both[:rows] + both[rows:] + part(left_high, right_low)


def spread(out_ref, value):
    for piece in range(out_ref.shape[0]):
        out_ref[piece] = value


def lane_ids():
    return lax.broadcasted_iota(jnp.int32, (8, LANES), 1)


def select_lanes(tiles, tile_at, lane_at):
    total = jnp.zeros((8, LANES), jnp.float32)
    for number, tile in enumerate(tiles):
        moved = jnp.take_along_axis(tile, lane_at, axis=1, mode="promise_in_bounds")
        total = jnp.where(tile_at == number, moved, total)
    return total


def row_of(index_ref, row):
    return jnp.broadcast_to(index_ref[row : row + 1, :], (8, LANES))


def sum_spread(parts_ref, out_ref):
    spread(out_ref, jnp.sum(parts_ref[...], axis=0))


def sum_only(parts_ref, out_ref):
    out_ref[...] = jnp.sum(parts_ref[...], axis=0)


def subtract_spread(parts_ref, kept_ref, out_ref):
    spread(out_ref, kept_ref[...] - jnp.sum(parts_ref[...], axis=0))


def sum_over_x(parts_ref):
    return [
        parts_ref[4 * i] + parts_ref[4 * i + 1] + parts_ref[4 * i + 2] + parts_ref[4 * i + 3]
        for i in range(8)
    ]


def regroup(sources):
    group = lane_ids() // 32
    total = jnp.zeros((8, LANES), jnp.float32)
    for to, (tile, start) in enumerate(sources):
        shift = ((to - start) * 32) % LANES
        moved = pltpu.roll(tile, shift, 1) if shift else tile
        total = jnp.where(group == to, moved, total)
    return total


def start(right_ref, root_ref, coupling_ref, out_ref, planes_ref):
    spread(out_ref, right_ref[...])
    planes_ref[:32] = root_ref[0]
    planes_ref[32:64] = root_ref[1]
    planes_ref[64:, :512] = coupling_ref[:32]
    planes_ref[64:, 512:] = coupling_ref[32:]


def lower_product(parts_ref, weights_ref, out_ref):
    x_at = lax.axis_index("x")
    operand = jnp.concatenate([parts_ref[x_at * 8 + i] for i in range(8)], axis=1)
    spread(out_ref, product(operand, weights_ref[...]))


def lower_product_copy(parts_ref, weights_ref, middle_ref, out_ref, copy_ref):
    lower_product(parts_ref, weights_ref, out_ref)
    copy_ref[...] = middle_ref[1]


def middle_product(parts_ref, weights_ref, out_ref):
    operand = jnp.concatenate([parts_ref[i] for i in range(8)], axis=1)
    doubled = jnp.concatenate([weights_ref[...], weights_ref[...]], axis=0)
    spread(out_ref, product(operand, doubled, True))


def extend(width, per_tile, parts_ref, weights_ref, source_ref, right_ref, out_ref, kept_ref):
    value = jnp.sum(parts_ref[...], axis=0)
    kept_ref[...] = value
    update = product(value[:, :width], weights_ref[...])
    tiles = [update[:, i * LANES : (i + 1) * LANES] for i in range(4)]
    for tile in range(32):
        source = row_of(source_ref, tile)
        out_ref[(tile % 8) * 4 + tile // 8] = -select_lanes(tiles, source >> 7, source & 127)
    if per_tile == 2:
        block_at = lax.axis_index(("b", "d", "y", "k"))
    else:
        block_at = lax.axis_index(("a", "b", "d", "y", "k"))
    tile_at = block_at // per_tile
    piece_at = (tile_at % 8) * 4 + tile_at // 8
    out_ref[piece_at] = out_ref[piece_at] + right_ref[...]


def stack_spread(parts_ref, kept_ref, out_ref):
    value = jnp.sum(parts_ref[...], axis=0)
    for piece in range(16):
        out_ref[piece, :8] = value
        out_ref[piece, 8:] = kept_ref[...]


def unstack_spread(parts_ref, out_ref, kept_ref):
    spread(out_ref, jnp.sum(parts_ref[:, :8, :], axis=0))
    first = lax.axis_index("a") * 8
    on = jnp.where(lax.axis_index("x") == 0, 1.0, 0.0)
    for tile in range(2):
        blocks = [parts_ref[first + tile * 4 + i, 8:, :] for i in range(4)]
        for half in range(2):
            kept_ref[half * 2 + tile] = on * regroup([(block, half) for block in blocks])


def root_first(parts_ref, weights_ref, out_ref):
    operand = jnp.concatenate([parts_ref[i] for i in range(8)], axis=1)
    for step in range(4):
        weights = weights_ref[step * 4 : step * 4 + 4, :32, :].reshape(LANES, QUARTER)
        value = product(operand, weights, True)
        for row in range(8):
            out_ref[row * 4 + step] = value


def spread_product(out_ref, operand, weights_at):
    for step in range(4):
        value = product(operand, weights_at(step).reshape(LANES, QUARTER), True)
        for piece in range(out_ref.shape[0]):
            out_ref[piece, :, step * LANES : (step + 1) * LANES] = value


def root_second(parts_ref, weights_ref, out_ref):
    rows = sum_over_x(parts_ref)
    tiles = [regroup([(rows[(i % 2) * 4 + t], i // 2) for t in range(4)]) for i in range(8)]
    operand = jnp.concatenate(tiles, axis=1)
    spread_product(out_ref, operand, lambda step: weights_ref[step * 4 : step * 4 + 4, 32:64, :])


def pick_middle(parts_ref, index_ref, kept_ref, weights_ref, out_ref, rows_ref):
    rows = sum_over_x(parts_ref)
    for i in range(8):
        rows_ref[i] = rows[i]
    tiles = [rows[i // 4][:, (i % 4) * LANES : (i % 4 + 1) * LANES] for i in range(32)]
    picked = []
    for i in range(4):
        at = row_of(index_ref, i)
        plane = at >> 8
        tile_at = ((at >> 5) & 7) * 4 + (plane >> 2)
        picked.append(select_lanes(tiles, tile_at, (plane & 3) * 32 + (at & 31)))
    operand = jnp.concatenate(picked, axis=1)
    values = []
    first = lax.axis_index("a") * 8
    for half in range(2):
        lanes = slice(half * 512, (half + 1) * 512)
        weights = weights_ref[pl.ds(first, 8), 64:96, lanes].reshape(256, 512)
        coupled = product(operand, weights, True)
        for tile in range(2):
            values.append(kept_ref[half * 2 + tile] - coupled[:, tile * LANES : (tile + 1) * LANES])
    for to in range(4):
        low, high = values[to // 2], values[2 + to // 2]
        start = (to % 2) * 2
        value = regroup([(low, start), (low, start + 1), (high, start), (high, start + 1)])
        for row in range(8):
            out_ref[row * 4 + to] = value


def middle_second(parts_ref, weights_ref, out_ref):
    rows = sum_over_x(parts_ref)
    tiles = []
    for i in range(8):
        pair = [rows[(i % 4) * 2], rows[(i % 4) * 2 + 1]]
        tiles.append(regroup([(pair[g // 2], (g % 2) * 2 + i // 4) for g in range(4)]))
    operand = jnp.concatenate(tiles, axis=1)
    spread_product(out_ref, operand, lambda step: weights_ref[step * 2 : step * 2 + 2])


def pick_lower(parts_ref, index_ref, weights_ref, out_ref, rows_ref):
    rows = sum_over_x(parts_ref)
    for i in range(8):
        rows_ref[i] = rows[i]
    tiles = [rows[i // 4][:, (i % 4) * LANES : (i % 4 + 1) * LANES] for i in range(32)]
    picked = []
    for i in range(4):
        at = row_of(index_ref, i)
        tile_at = ((at >> 6) & 7) * 4 + (at >> 10)
        picked.append(select_lanes(tiles, tile_at, ((at >> 9) & 1) * 64 + (at & 63)))
    spread(out_ref, product(jnp.concatenate(picked, axis=1), weights_ref[...]))


def sources(positions):
    numbers = jnp.arange(512, dtype=jnp.int32)[:, None]
    hit = positions[:, None] == jnp.arange(S, dtype=jnp.int32)[None, :]
    return jnp.max(jnp.where(hit, numbers, -1), axis=0).reshape(32, LANES)


def placed(right_block, at):
    width = right_block.shape[1]
    times = LANES // width
    lanes = jnp.arange(LANES, dtype=jnp.int32)[None, :] // width
    here = (lanes == at % times) & (lax.axis_index("x") == 0)
    return jnp.where(here, jnp.tile(right_block, (1, times)), 0.0)


def local(
    right_root,
    right_middle,
    right_lower,
    inverse_root,
    inverse_middle,
    inverse_lower,
    upward_middle,
    upward_lower,
    downward_middle,
    downward_lower,
    index_middle,
    index_lower,
):
    at = lax.axis_index
    n = ("a", "b", "d", "y", "k")
    positions_middle = lax.dynamic_index_in_dim(index_middle, at("a"), 0, keepdims=False)
    positions_lower = lax.dynamic_index_in_dim(index_lower, at(("a", "b")), 0, keepdims=False)
    right_middle_tile = placed(right_middle, at(("b", "d", "y", "k")))
    right_root_tile = placed(right_root, at(n))
    source_lower = sources(positions_lower)
    source_middle = sources(positions_middle)

    parts, planes = call(
        start,
        [(32, 8, 128), (96, QUARTER)],
        right_lower,
        inverse_root.transpose(0, 2, 1),
        downward_middle.T,
    )
    planes = lax.all_gather(planes, ("a", "b", "d"), axis=0)

    parts = exchange(parts, "dyk")
    parts, middle_planes = call(
        lower_product_copy,
        [(4, 8, 128), (64, QUARTER)],
        parts,
        inverse_lower[0],
        inverse_middle.transpose(0, 2, 1),
        after=(source_lower, right_middle_tile),
    )
    middle_planes = lax.all_gather(middle_planes, ("b", "d"), axis=0)
    parts = exchange(parts, "x")
    parts, z_lower = call(
        functools.partial(extend, 128, 2),
        [(32, 8, 128), (8, 128)],
        parts,
        upward_lower,
        source_lower,
        right_middle_tile,
    )
    parts = exchange(parts, "ykx")
    parts = exchange(call(sum_spread, [(8, 8, 128)], parts), "bd")
    parts = exchange(call(sum_spread, [(8, 8, 128)], parts), "yk")
    parts = exchange(call(middle_product, [(4, 8, 128)], parts, inverse_middle[0].T), "x")
    parts, z_middle = call(
        functools.partial(extend, 64, 4),
        [(32, 8, 128), (8, 128)],
        parts,
        upward_middle,
        source_middle,
        right_root_tile,
    )
    parts = exchange(parts, "ykx")
    parts = exchange(call(stack_spread, [(16, 16, 128)], parts, z_middle), "abd")
    parts, z_middle = call(unstack_spread, [(8, 8, 128), (4, 8, 128)], parts, after=(planes[0, :8, :128],))
    parts = exchange(parts, "yk")
    parts = exchange(call(root_first, [(32, 8, 128)], parts, planes), "ykx")
    parts = exchange(call(root_second, [(32, 8, 512)], parts, planes), "ykx")
    parts, rows = call(
        pick_middle,
        [(32, 8, 128), (8, 8, 512)],
        parts,
        positions_middle.reshape(4, LANES),
        z_middle,
        planes,
    )
    row = lax.dynamic_index_in_dim(rows, at(("y", "k")), 0, keepdims=False)
    solution_root = lax.dynamic_slice_in_dim(row, at(("a", "b", "d")) * 32, 32, 1)
    parts = exchange(parts, "ykx")
    parts = exchange(call(middle_second, [(32, 8, 512)], parts, middle_planes), "ykx")
    parts, rows = call(
        pick_lower,
        [(4, 8, 128), (8, 8, 512)],
        parts,
        positions_lower.reshape(4, LANES),
        downward_lower,
    )
    row = lax.dynamic_index_in_dim(rows, at(("y", "k")), 0, keepdims=False)
    solution_middle = lax.dynamic_slice_in_dim(row, at(("b", "d")) * 64, 64, 1)
    parts = exchange(parts, "x")
    parts = exchange(call(subtract_spread, [(32, 8, 128)], parts, z_lower), "dyk")
    parts = exchange(call(lower_product, [(4, 8, 128)], parts, inverse_lower[1]), "x")
    solution_lower = call(sum_only, [(8, 128)], parts)
    return (solution_root, solution_middle, solution_lower)


def solution(mesh):
    split = Mesh(mesh.devices.reshape(tuple(SIZES.values())), tuple(SIZES))
    n = ("a", "b", "d", "y", "k")
    in_specs = (
        P(None, n),
        P(None, n),
        P(None, n),
        P(None, "x", n),
        P(None, "x", n),
        P(None, "x", n),
        P(n, "x"),
        P(n, "x"),
        P("x", n),
        P("x", n),
        P(None, "x"),
        P(None, "x"),
    )
    out_specs = (P(None, n), P(None, n), P(None, n))
    return jax.shard_map(local, mesh=split, in_specs=in_specs, out_specs=out_specs, check_vma=False)
```

```python
import jax
import jax.numpy as jnp
from jax import lax
from jax.experimental import pallas as pl
from jax.experimental.pallas import tpu as pltpu
from jax.sharding import Mesh
from jax.sharding import PartitionSpec as P

S = 4096
QUARTER = 1024
LANES = 128
SIZES = {"a": 2, "b": 2, "d": 4, "y": 4, "k": 2, "x": 4}
VMEM_LIMIT = 32 * 1024 * 1024


def count(axes):
    total = 1
    for axis in axes:
        total *= SIZES[axis]
    return total


def exchange(pieces, axes):
    return lax.all_to_all(pieces, tuple(axes), 0, 0, tiled=False)


def call(body, out_shapes, *operands, after=()):
    shapes = [jax.ShapeDtypeStruct(shape, jnp.float32) for shape in out_shapes]
    whole = pl.BlockSpec(memory_space=pltpu.VMEM)
    extra = len(after)
    return pl.pallas_call(
        lambda *refs: body(*refs[extra:]),
        out_shape=shapes[0] if len(shapes) == 1 else tuple(shapes),
        in_specs=[pl.BlockSpec(memory_space=pl.ANY)] * extra + [whole] * len(operands),
        out_specs=whole if len(shapes) == 1 else (whole,) * len(shapes),
        compiler_params=pltpu.CompilerParams(vmem_limit_bytes=VMEM_LIMIT),
    )(*after, *operands)


def product(left_side, right_side, transposed=False):
    def part(one, two):
        dims = (((1,), (1 if transposed else 0,)), ((), ()))
        return lax.dot_general(one, two, dims, preferred_element_type=jnp.float32)

    rows = left_side.shape[0]
    left_high = left_side.astype(jnp.bfloat16)
    left_low = (left_side - left_high.astype(jnp.float32)).astype(jnp.bfloat16)
    right_high = right_side.astype(jnp.bfloat16)
    right_low = (right_side - right_high.astype(jnp.float32)).astype(jnp.bfloat16)
    both = part(jnp.concatenate([left_high, left_low], axis=0), right_high)
    return both[:rows] + both[rows:] + part(left_high, right_low)


def spread(out_ref, value):
    for piece in range(out_ref.shape[0]):
        out_ref[piece] = value


def lane_ids():
    return lax.broadcasted_iota(jnp.int32, (8, LANES), 1)


def select_lanes(tiles, tile_at, lane_at):
    total = jnp.zeros((8, LANES), jnp.float32)
    for number, tile in enumerate(tiles):
        moved = jnp.take_along_axis(tile, lane_at, axis=1, mode="promise_in_bounds")
        total = jnp.where(tile_at == number, moved, total)
    return total


def row_of(index_ref, row):
    return jnp.broadcast_to(index_ref[row : row + 1, :], (8, LANES))


def sum_spread(parts_ref, out_ref):
    spread(out_ref, jnp.sum(parts_ref[...], axis=0))


def sum_only(parts_ref, out_ref):
    out_ref[...] = jnp.sum(parts_ref[...], axis=0)


def subtract_spread(parts_ref, kept_ref, out_ref):
    spread(out_ref, kept_ref[...] - jnp.sum(parts_ref[...], axis=0))


def sum_over_x(parts_ref):
    return [
        parts_ref[4 * i] + parts_ref[4 * i + 1] + parts_ref[4 * i + 2] + parts_ref[4 * i + 3]
        for i in range(8)
    ]


def regroup(sources):
    group = lane_ids() // 32
    total = jnp.zeros((8, LANES), jnp.float32)
    for to, (tile, start) in enumerate(sources):
        shift = ((to - start) * 32) % LANES
        moved = pltpu.roll(tile, shift, 1) if shift else tile
        total = jnp.where(group == to, moved, total)
    return total


def carve(planes_ref, first_ref, second_ref, coupling_ref):
    first_ref[...] = planes_ref[:, :32, :]
    second_ref[...] = planes_ref[:, 32:64, :]
    coupling_ref[...] = planes_ref[pl.ds(lax.axis_index("a") * 8, 8), 64:, :]


def hold(weights_ref, out_ref):
    out_ref[...] = weights_ref[...]


def start(right_ref, root_ref, coupling_ref, out_ref, planes_ref):
    spread(out_ref, right_ref[...])
    planes_ref[:32] = root_ref[0]
    planes_ref[32:64] = root_ref[1]
    planes_ref[64:, :512] = coupling_ref[:32]
    planes_ref[64:, 512:] = coupling_ref[32:]


def lower_product(parts_ref, weights_ref, out_ref):
    x_at = lax.axis_index("x")
    operand = jnp.concatenate([parts_ref[x_at * 8 + i] for i in range(8)], axis=1)
    spread(out_ref, product(operand, weights_ref[...]))


def lower_product_first(parts_ref, weights_ref, middle_ref, upward_ref, source_ref, out_ref, copy_ref):
    copy_ref[...] = middle_ref[1]
    x_at = lax.axis_index("x")
    operand = jnp.concatenate([parts_ref[x_at * 8 + i] for i in range(8)], axis=1)
    value = product(operand, weights_ref[...])
    source = source_ref[...].astype(jnp.float32)
    for to in range(4):
        out_ref[to, :8] = value
        for tile in range(4):
            rows = slice(8 + 64 * tile, 8 + 64 * (tile + 1))
            out_ref[to, rows] = upward_ref[:, tile * LANES : (tile + 1) * LANES]
        out_ref[to, 264:] = source


def extend(tiles, sources, block_at, per_tile, right_ref, out_ref):
    for tile in range(32):
        source = jnp.broadcast_to(sources[tile : tile + 1], (8, LANES))
        out_ref[(tile % 8) * 4 + tile // 8] = -select_lanes(tiles, source >> 7, source & 127)
    tile_at = block_at // per_tile
    piece_at = (tile_at % 8) * 4 + tile_at // 8
    out_ref[piece_at] = out_ref[piece_at] + right_ref[...]


def lower_extend(parts_ref, weights_ref, source_ref, right_ref, out_ref, kept_ref):
    value = jnp.sum(parts_ref[:, :8, :], axis=0)
    kept_ref[...] = value
    update = product(value, weights_ref[...])
    tiles = [update[:, i * LANES : (i + 1) * LANES] for i in range(4)]
    extend(tiles, source_ref[...], lax.axis_index(("b", "d", "y", "k")), 2, right_ref, out_ref)


def middle_extend(parts_ref, weights_ref, moved_ref, right_ref, out_ref, kept_ref):
    operand = jnp.concatenate([parts_ref[i] for i in range(8)], axis=1)
    doubled = jnp.concatenate([weights_ref[...], weights_ref[...]], axis=0)
    value = product(operand, doubled, True)
    kept_ref[...] = value
    tiles = []
    sources = jnp.full((32, LANES), -1.0, jnp.float32)
    for x in range(4):
        upward = [moved_ref[x, 8 + 64 * tile : 8 + 64 * (tile + 1), :] for tile in range(4)]
        update = product(value[:, :64], jnp.concatenate(upward, axis=1))
        tiles += [update[:, i * LANES : (i + 1) * LANES] for i in range(4)]
        number = moved_ref[x, 264:, :]
        sources = jnp.maximum(sources, jnp.where(number >= 0, number + 512.0 * x, -1.0))
    sources = sources.astype(jnp.int32)
    extend(tiles, sources, lax.axis_index(("a", "b", "d", "y", "k")), 4, right_ref, out_ref)


def stack_spread(parts_ref, kept_ref, out_ref):
    value = jnp.sum(parts_ref[...], axis=0)
    for piece in range(16):
        out_ref[piece, :8] = value
        out_ref[piece, 8:] = kept_ref[...]


def unstack_spread(parts_ref, out_ref, kept_ref):
    spread(out_ref, jnp.sum(parts_ref[:, :8, :], axis=0))
    first = lax.axis_index("a") * 8
    for tile in range(2):
        blocks = [parts_ref[first + tile * 4 + i, 8:, :] for i in range(4)]
        for half in range(2):
            kept_ref[half * 2 + tile] = regroup([(block, half) for block in blocks])


def root_first(parts_ref, weights_ref, out_ref):
    operand = jnp.concatenate([parts_ref[i] for i in range(8)], axis=1)
    for step in range(4):
        weights = weights_ref[step * 4 : step * 4 + 4].reshape(LANES, QUARTER)
        value = product(operand, weights, True)
        for row in range(8):
            out_ref[row * 4 + step] = value


def spread_product(out_ref, operand, weights_at):
    for step in range(4):
        value = product(operand, weights_at(step).reshape(LANES, QUARTER), True)
        for piece in range(out_ref.shape[0]):
            out_ref[piece, :, step * LANES : (step + 1) * LANES] = value


def root_second(parts_ref, weights_ref, out_ref):
    rows = sum_over_x(parts_ref)
    tiles = [regroup([(rows[(i % 2) * 4 + t], i // 2) for t in range(4)]) for i in range(8)]
    operand = jnp.concatenate(tiles, axis=1)
    spread_product(out_ref, operand, lambda step: weights_ref[step * 4 : step * 4 + 4])


def pick_middle(parts_ref, index_ref, kept_ref, weights_ref, out_ref, rows_ref):
    rows = sum_over_x(parts_ref)
    for i in range(8):
        rows_ref[i] = rows[i]
    tiles = [rows[i // 4][:, (i % 4) * LANES : (i % 4 + 1) * LANES] for i in range(32)]
    picked = []
    for i in range(4):
        at = row_of(index_ref, i)
        plane = at >> 8
        tile_at = ((at >> 5) & 7) * 4 + (plane >> 2)
        picked.append(select_lanes(tiles, tile_at, (plane & 3) * 32 + (at & 31)))
    operand = jnp.concatenate(picked, axis=1)
    values = []
    for half in range(2):
        weights = weights_ref[:, :, half * 512 : (half + 1) * 512].reshape(256, 512)
        coupled = product(operand, weights, True)
        for tile in range(2):
            values.append(kept_ref[half * 2 + tile] - coupled[:, tile * LANES : (tile + 1) * LANES])
    for to in range(4):
        low, high = values[to // 2], values[2 + to // 2]
        start = (to % 2) * 2
        value = regroup([(low, start), (low, start + 1), (high, start), (high, start + 1)])
        for row in range(8):
            out_ref[row * 4 + to] = value


def middle_second(parts_ref, weights_ref, out_ref):
    rows = sum_over_x(parts_ref)
    tiles = []
    for i in range(8):
        pair = [rows[(i % 4) * 2], rows[(i % 4) * 2 + 1]]
        tiles.append(regroup([(pair[g // 2], (g % 2) * 2 + i // 4) for g in range(4)]))
    operand = jnp.concatenate(tiles, axis=1)
    spread_product(out_ref, operand, lambda step: weights_ref[step * 2 : step * 2 + 2])


def pick_lower(parts_ref, index_ref, weights_ref, out_ref, rows_ref):
    rows = sum_over_x(parts_ref)
    for i in range(8):
        rows_ref[i] = rows[i]
    tiles = [rows[i // 4][:, (i % 4) * LANES : (i % 4 + 1) * LANES] for i in range(32)]
    picked = []
    for i in range(4):
        at = row_of(index_ref, i)
        tile_at = ((at >> 6) & 7) * 4 + (at >> 10)
        picked.append(select_lanes(tiles, tile_at, ((at >> 9) & 1) * 64 + (at & 63)))
    spread(out_ref, product(jnp.concatenate(picked, axis=1), weights_ref[...]))


def sources(positions):
    numbers = jnp.arange(512, dtype=jnp.int32)[:, None]
    hit = positions[:, None] == jnp.arange(S, dtype=jnp.int32)[None, :]
    return jnp.max(jnp.where(hit, numbers, -1), axis=0).reshape(32, LANES)


def placed(right_block, at):
    width = right_block.shape[1]
    times = LANES // width
    lanes = jnp.arange(LANES, dtype=jnp.int32)[None, :] // width
    here = (lanes == at % times) & (lax.axis_index("x") == 0)
    return jnp.where(here, jnp.tile(right_block, (1, times)), 0.0)


def local(
    right_root,
    right_middle,
    right_lower,
    inverse_root,
    inverse_middle,
    inverse_lower,
    upward_middle,
    upward_lower,
    downward_middle,
    downward_lower,
    index_middle,
    index_lower,
):
    at = lax.axis_index
    n = ("a", "b", "d", "y", "k")
    positions_middle = lax.dynamic_index_in_dim(index_middle, at("a"), 0, keepdims=False)
    positions_lower = lax.dynamic_index_in_dim(index_lower, at(("a", "b")), 0, keepdims=False)
    right_middle_tile = placed(right_middle, at(("b", "d", "y", "k")))
    right_root_tile = placed(right_root, at(n))
    source_lower = sources(positions_lower)
    source_middle = sources(positions_middle)

    parts, planes = call(
        start,
        [(32, 8, 128), (96, QUARTER)],
        right_lower,
        inverse_root.transpose(0, 2, 1),
        downward_middle.T,
    )
    planes = lax.all_gather(planes, ("a", "b", "d"), axis=0)

    parts = exchange(parts, "dyk")
    moved, middle_planes = call(
        lower_product_first,
        [(4, 296, 128), (64, QUARTER)],
        parts,
        inverse_lower[0],
        inverse_middle.transpose(0, 2, 1),
        upward_middle,
        source_middle,
        after=(source_lower, right_middle_tile),
    )
    middle_planes = lax.all_gather(middle_planes, ("b", "d"), axis=0)
    moved = exchange(moved, "x")
    parts, z_lower = call(
        lower_extend, [(32, 8, 128), (8, 128)], moved, upward_lower, source_lower, right_middle_tile
    )
    parts = exchange(parts, "ykx")
    parts = exchange(call(sum_spread, [(8, 8, 128)], parts), "bd")
    parts = exchange(call(sum_spread, [(8, 8, 128)], parts), "yk")
    parts, z_middle = call(
        middle_extend,
        [(32, 8, 128), (8, 128)],
        parts,
        inverse_middle[0].T,
        moved,
        right_root_tile,
    )
    parts = exchange(parts, "ykx")
    parts = exchange(call(stack_spread, [(16, 16, 128)], parts, z_middle), "abd")
    first_weights, second_weights, coupling = call(
        carve, [(16, 32, QUARTER), (16, 32, QUARTER), (8, 32, QUARTER)], planes
    )
    parts, z_middle = call(unstack_spread, [(8, 8, 128), (4, 8, 128)], parts, after=(first_weights,))
    parts = exchange(parts, "yk")
    parts = exchange(call(root_first, [(32, 8, 128)], parts, first_weights), "ykx")
    parts = exchange(call(root_second, [(32, 8, 512)], parts, second_weights), "ykx")
    parts, rows = call(
        pick_middle,
        [(32, 8, 128), (8, 8, 512)],
        parts,
        positions_middle.reshape(4, LANES),
        z_middle,
        coupling,
    )
    row = lax.dynamic_index_in_dim(rows, at(("y", "k")), 0, keepdims=False)
    solution_root = lax.dynamic_slice_in_dim(row, at(("a", "b", "d")) * 32, 32, 1)
    parts = exchange(parts, "ykx")
    middle_planes = call(hold, [(8, 64, QUARTER)], middle_planes)
    parts = exchange(call(middle_second, [(32, 8, 512)], parts, middle_planes), "ykx")
    parts, rows = call(
        pick_lower,
        [(4, 8, 128), (8, 8, 512)],
        parts,
        positions_lower.reshape(4, LANES),
        downward_lower,
    )
    row = lax.dynamic_index_in_dim(rows, at(("y", "k")), 0, keepdims=False)
    solution_middle = lax.dynamic_slice_in_dim(row, at(("b", "d")) * 64, 64, 1)
    parts = exchange(parts, "x")
    parts = exchange(call(subtract_spread, [(32, 8, 128)], parts, z_lower), "dyk")
    parts = exchange(call(lower_product, [(4, 8, 128)], parts, inverse_lower[1]), "x")
    solution_lower = call(sum_only, [(8, 128)], parts)
    return (solution_root, solution_middle, solution_lower)


def solution(mesh):
    split = Mesh(mesh.devices.reshape(tuple(SIZES.values())), tuple(SIZES))
    n = ("a", "b", "d", "y", "k")
    in_specs = (
        P(None, n),
        P(None, n),
        P(None, n),
        P(None, "x", n),
        P(None, "x", n),
        P(None, "x", n),
        P(n, "x"),
        P(n, "x"),
        P("x", n),
        P("x", n),
        P(None, "x"),
        P(None, "x"),
    )
    out_specs = (P(None, n), P(None, n), P(None, n))
    return jax.shard_map(local, mesh=split, in_specs=in_specs, out_specs=out_specs, check_vma=False)
```

```python
import jax
import jax.numpy as jnp
from jax import lax
from jax.experimental import pallas as pl
from jax.experimental.pallas import tpu as pltpu
from jax.sharding import Mesh
from jax.sharding import PartitionSpec as P

S = 4096
QUARTER = 1024
LANES = 128
SIZES = {"a": 2, "b": 2, "d": 4, "y": 4, "k": 2, "x": 4}
VMEM_LIMIT = 32 * 1024 * 1024


def count(axes):
    total = 1
    for axis in axes:
        total *= SIZES[axis]
    return total


def exchange(pieces, axes):
    return lax.all_to_all(pieces, tuple(axes), 0, 0, tiled=False)


def call(body, out_shapes, *operands, after=()):
    shapes = [jax.ShapeDtypeStruct(shape, jnp.float32) for shape in out_shapes]
    whole = pl.BlockSpec(memory_space=pltpu.VMEM)
    extra = len(after)
    return pl.pallas_call(
        lambda *refs: body(*refs[extra:]),
        out_shape=shapes[0] if len(shapes) == 1 else tuple(shapes),
        in_specs=[pl.BlockSpec(memory_space=pl.ANY)] * extra + [whole] * len(operands),
        out_specs=whole if len(shapes) == 1 else (whole,) * len(shapes),
        compiler_params=pltpu.CompilerParams(vmem_limit_bytes=VMEM_LIMIT),
    )(*after, *operands)


def product(left_side, right_side, transposed=False):
    def part(one, two):
        dims = (((1,), (1 if transposed else 0,)), ((), ()))
        return lax.dot_general(one, two, dims, preferred_element_type=jnp.float32)

    rows = left_side.shape[0]
    left_high = left_side.astype(jnp.bfloat16)
    left_low = (left_side - left_high.astype(jnp.float32)).astype(jnp.bfloat16)
    right_high = right_side.astype(jnp.bfloat16)
    right_low = (right_side - right_high.astype(jnp.float32)).astype(jnp.bfloat16)
    both = part(jnp.concatenate([left_high, left_low], axis=0), right_high)
    return both[:rows] + both[rows:] + part(left_high, right_low)


def spread(out_ref, value):
    for piece in range(out_ref.shape[0]):
        out_ref[piece] = value


def lane_ids():
    return lax.broadcasted_iota(jnp.int32, (8, LANES), 1)


def select_lanes(tiles, tile_at, lane_at):
    total = jnp.zeros((8, LANES), jnp.float32)
    for number, tile in enumerate(tiles):
        moved = jnp.take_along_axis(tile, lane_at, axis=1, mode="promise_in_bounds")
        total = jnp.where(tile_at == number, moved, total)
    return total


def row_of(index_ref, row):
    return jnp.broadcast_to(index_ref[row : row + 1, :], (8, LANES))


def sum_spread(parts_ref, out_ref):
    spread(out_ref, jnp.sum(parts_ref[...], axis=0))


def sum_only(parts_ref, out_ref):
    out_ref[...] = jnp.sum(parts_ref[...], axis=0)


def subtract_spread(parts_ref, kept_ref, out_ref):
    spread(out_ref, kept_ref[...] - jnp.sum(parts_ref[...], axis=0))


def sum_over_x(parts_ref):
    return [
        parts_ref[4 * i] + parts_ref[4 * i + 1] + parts_ref[4 * i + 2] + parts_ref[4 * i + 3]
        for i in range(8)
    ]


def regroup(sources):
    group = lane_ids() // 32
    total = jnp.zeros((8, LANES), jnp.float32)
    for to, (tile, start) in enumerate(sources):
        shift = ((to - start) * 32) % LANES
        moved = pltpu.roll(tile, shift, 1) if shift else tile
        total = jnp.where(group == to, moved, total)
    return total


def carve(planes_ref, first_ref, second_ref, coupling_ref):
    first_ref[...] = planes_ref[:, :32, :]
    second_ref[...] = planes_ref[:, 32:64, :]
    coupling_ref[...] = planes_ref[pl.ds(lax.axis_index("a") * 8, 8), 64:, :]


def hold(weights_ref, out_ref):
    out_ref[...] = weights_ref[...]


def stack_planes(root_ref, coupling_ref, planes_ref):
    planes_ref[:32] = root_ref[0]
    planes_ref[32:64] = root_ref[1]
    planes_ref[64:, :512] = coupling_ref[:32]
    planes_ref[64:, 512:] = coupling_ref[32:]


def spread_right(right_ref, out_ref):
    spread(out_ref, right_ref[...])


def map_sources(lower_ref, middle_ref, lower_out_ref, middle_out_ref):
    for index_ref, out_ref in ((lower_ref, lower_out_ref), (middle_ref, middle_out_ref)):
        index = jnp.concatenate([index_ref[i : i + 1, :] for i in range(4)], axis=1)
        number = lax.broadcasted_iota(jnp.int32, (32, 512), 1) + 1
        rows = jnp.broadcast_to(index >> 7, (32, 512)) == lax.broadcasted_iota(jnp.int32, (32, 512), 0)
        lanes = jnp.broadcast_to(index & 127, (LANES, 512)) == lax.broadcasted_iota(jnp.int32, (LANES, 512), 0)
        parts = [jnp.where(rows, part, 0).astype(jnp.float32) for part in (number >> 4, number & 15)]
        found = lax.dot_general(
            jnp.concatenate(parts, axis=0).astype(jnp.bfloat16),
            jnp.where(lanes, 1.0, 0.0).astype(jnp.bfloat16),
            (((1,), (1,)), ((), ())),
            preferred_element_type=jnp.float32,
        )
        out_ref[...] = found[:32] * 16.0 + found[32:] - 1.0


def hold_two(middle_ref, upward_ref, middle_out_ref, upward_out_ref):
    middle_out_ref[...] = middle_ref[1]
    upward_out_ref[...] = upward_ref[...]


def lower_product(parts_ref, weights_ref, out_ref):
    x_at = lax.axis_index("x")
    operand = jnp.concatenate([parts_ref[x_at * 8 + i] for i in range(8)], axis=1)
    spread(out_ref, product(operand, weights_ref[...]))


def lower_product_first(parts_ref, weights_ref, middle_ref, upward_ref, source_ref, out_ref, copy_ref):
    copy_ref[...] = middle_ref[...]
    x_at = lax.axis_index("x")
    operand = jnp.concatenate([parts_ref[x_at * 8 + i] for i in range(8)], axis=1)
    value = product(operand, weights_ref[...])
    source = source_ref[...]
    for to in range(4):
        out_ref[to, :8] = value
        for tile in range(4):
            rows = slice(8 + 64 * tile, 8 + 64 * (tile + 1))
            out_ref[to, rows] = upward_ref[:, tile * LANES : (tile + 1) * LANES]
        out_ref[to, 264:] = source


def extend(tiles, sources, block_at, per_tile, right_ref, out_ref):
    for tile in range(32):
        source = jnp.broadcast_to(sources[tile : tile + 1], (8, LANES))
        out_ref[(tile % 8) * 4 + tile // 8] = -select_lanes(tiles, source >> 7, source & 127)
    tile_at = block_at // per_tile
    piece_at = (tile_at % 8) * 4 + tile_at // 8
    out_ref[piece_at] = out_ref[piece_at] + right_ref[...]


def lower_extend(parts_ref, weights_ref, source_ref, right_ref, out_ref, kept_ref):
    value = jnp.sum(parts_ref[:, :8, :], axis=0)
    kept_ref[...] = value
    update = product(value, weights_ref[...])
    tiles = [update[:, i * LANES : (i + 1) * LANES] for i in range(4)]
    extend(tiles, source_ref[...].astype(jnp.int32), lax.axis_index(("b", "d", "y", "k")), 2, right_ref, out_ref)


def middle_extend(parts_ref, weights_ref, moved_ref, right_ref, out_ref, kept_ref):
    operand = jnp.concatenate([parts_ref[i] for i in range(8)], axis=1)
    doubled = jnp.concatenate([weights_ref[...], weights_ref[...]], axis=0)
    value = product(operand, doubled, True)
    kept_ref[...] = value
    tiles = []
    sources = jnp.full((32, LANES), -1.0, jnp.float32)
    for x in range(4):
        upward = [moved_ref[x, 8 + 64 * tile : 8 + 64 * (tile + 1), :] for tile in range(4)]
        update = product(value[:, :64], jnp.concatenate(upward, axis=1))
        tiles += [update[:, i * LANES : (i + 1) * LANES] for i in range(4)]
        number = moved_ref[x, 264:, :]
        sources = jnp.maximum(sources, jnp.where(number >= 0, number + 512.0 * x, -1.0))
    sources = sources.astype(jnp.int32)
    extend(tiles, sources, lax.axis_index(("a", "b", "d", "y", "k")), 4, right_ref, out_ref)


def stack_spread(parts_ref, kept_ref, out_ref):
    value = jnp.sum(parts_ref[...], axis=0)
    for piece in range(16):
        out_ref[piece, :8] = value
        out_ref[piece, 8:] = kept_ref[...]


def unstack_spread(parts_ref, out_ref, kept_ref):
    spread(out_ref, jnp.sum(parts_ref[:, :8, :], axis=0))
    first = lax.axis_index("a") * 8
    for tile in range(2):
        blocks = [parts_ref[first + tile * 4 + i, 8:, :] for i in range(4)]
        for half in range(2):
            kept_ref[half * 2 + tile] = regroup([(block, half) for block in blocks])


def root_first(parts_ref, weights_ref, out_ref):
    operand = jnp.concatenate([parts_ref[i] for i in range(8)], axis=1)
    for step in range(4):
        weights = weights_ref[step * 4 : step * 4 + 4].reshape(LANES, QUARTER)
        value = product(operand, weights, True)
        for row in range(8):
            out_ref[row * 4 + step] = value


def spread_product(out_ref, operand, weights_at):
    for step in range(4):
        value = product(operand, weights_at(step).reshape(LANES, QUARTER), True)
        for piece in range(out_ref.shape[0]):
            out_ref[piece, :, step * LANES : (step + 1) * LANES] = value


def root_second(parts_ref, weights_ref, out_ref):
    rows = sum_over_x(parts_ref)
    tiles = [regroup([(rows[(i % 2) * 4 + t], i // 2) for t in range(4)]) for i in range(8)]
    operand = jnp.concatenate(tiles, axis=1)
    spread_product(out_ref, operand, lambda step: weights_ref[step * 4 : step * 4 + 4])


def pick_middle(parts_ref, index_ref, kept_ref, weights_ref, out_ref, rows_ref):
    rows = sum_over_x(parts_ref)
    for i in range(8):
        rows_ref[i] = rows[i]
    tiles = [rows[i // 4][:, (i % 4) * LANES : (i % 4 + 1) * LANES] for i in range(32)]
    picked = []
    for i in range(4):
        at = row_of(index_ref, i)
        plane = at >> 8
        tile_at = ((at >> 5) & 7) * 4 + (plane >> 2)
        picked.append(select_lanes(tiles, tile_at, (plane & 3) * 32 + (at & 31)))
    operand = jnp.concatenate(picked, axis=1)
    values = []
    for half in range(2):
        weights = weights_ref[:, :, half * 512 : (half + 1) * 512].reshape(256, 512)
        coupled = product(operand, weights, True)
        for tile in range(2):
            values.append(kept_ref[half * 2 + tile] - coupled[:, tile * LANES : (tile + 1) * LANES])
    for to in range(4):
        low, high = values[to // 2], values[2 + to // 2]
        start = (to % 2) * 2
        value = regroup([(low, start), (low, start + 1), (high, start), (high, start + 1)])
        for row in range(8):
            out_ref[row * 4 + to] = value


def middle_second(parts_ref, weights_ref, out_ref):
    rows = sum_over_x(parts_ref)
    tiles = []
    for i in range(8):
        pair = [rows[(i % 4) * 2], rows[(i % 4) * 2 + 1]]
        tiles.append(regroup([(pair[g // 2], (g % 2) * 2 + i // 4) for g in range(4)]))
    operand = jnp.concatenate(tiles, axis=1)
    spread_product(out_ref, operand, lambda step: weights_ref[step * 2 : step * 2 + 2])


def pick_lower(parts_ref, index_ref, weights_ref, out_ref, rows_ref):
    rows = sum_over_x(parts_ref)
    for i in range(8):
        rows_ref[i] = rows[i]
    tiles = [rows[i // 4][:, (i % 4) * LANES : (i % 4 + 1) * LANES] for i in range(32)]
    picked = []
    for i in range(4):
        at = row_of(index_ref, i)
        tile_at = ((at >> 6) & 7) * 4 + (at >> 10)
        picked.append(select_lanes(tiles, tile_at, ((at >> 9) & 1) * 64 + (at & 63)))
    spread(out_ref, product(jnp.concatenate(picked, axis=1), weights_ref[...]))


def placed(right_block, at):
    width = right_block.shape[1]
    times = LANES // width
    lanes = jnp.arange(LANES, dtype=jnp.int32)[None, :] // width
    here = (lanes == at % times) & (lax.axis_index("x") == 0)
    return jnp.where(here, jnp.tile(right_block, (1, times)), 0.0)


def local(
    right_root,
    right_middle,
    right_lower,
    inverse_root,
    inverse_middle,
    inverse_lower,
    upward_middle,
    upward_lower,
    downward_middle,
    downward_lower,
    index_middle,
    index_lower,
):
    at = lax.axis_index
    n = ("a", "b", "d", "y", "k")
    positions_middle = lax.dynamic_index_in_dim(index_middle, at("a"), 0, keepdims=False)
    positions_lower = lax.dynamic_index_in_dim(index_lower, at(("a", "b")), 0, keepdims=False)
    right_middle_tile = placed(right_middle, at(("b", "d", "y", "k")))
    right_root_tile = placed(right_root, at(n))
    source_lower, source_middle = call(
        map_sources,
        [(32, LANES), (32, LANES)],
        positions_lower.reshape(4, LANES),
        positions_middle.reshape(4, LANES),
    )

    planes = call(stack_planes, [(96, QUARTER)], inverse_root.transpose(0, 2, 1), downward_middle.T)
    parts = call(spread_right, [(32, 8, 128)], right_lower, after=(planes,))
    planes = lax.all_gather(planes, ("a", "b", "d"), axis=0)

    parts = exchange(parts, "dyk")
    middle_own, upward_own = call(
        hold_two,
        [(64, QUARTER), (64, 512)],
        inverse_middle.transpose(0, 2, 1),
        upward_middle,
        after=(source_lower,),
    )
    moved, middle_planes = call(
        lower_product_first,
        [(4, 296, 128), (64, QUARTER)],
        parts,
        inverse_lower[0],
        middle_own,
        upward_own,
        source_middle,
        after=(source_lower, right_middle_tile),
    )
    middle_planes = lax.all_gather(middle_planes, ("b", "d"), axis=0)
    moved = exchange(moved, "x")
    parts, z_lower = call(
        lower_extend, [(32, 8, 128), (8, 128)], moved, upward_lower, source_lower, right_middle_tile
    )
    parts = exchange(parts, "ykx")
    parts = exchange(call(sum_spread, [(8, 8, 128)], parts), "bd")
    parts = exchange(call(sum_spread, [(8, 8, 128)], parts), "yk")
    parts, z_middle = call(
        middle_extend,
        [(32, 8, 128), (8, 128)],
        parts,
        inverse_middle[0].T,
        moved,
        right_root_tile,
    )
    parts = exchange(parts, "ykx")
    parts = exchange(call(stack_spread, [(16, 16, 128)], parts, z_middle), "abd")
    first_weights, second_weights, coupling = call(
        carve, [(16, 32, QUARTER), (16, 32, QUARTER), (8, 32, QUARTER)], planes
    )
    parts, z_middle = call(unstack_spread, [(8, 8, 128), (4, 8, 128)], parts, after=(first_weights,))
    parts = exchange(parts, "yk")
    parts = exchange(call(root_first, [(32, 8, 128)], parts, first_weights), "ykx")
    parts = exchange(call(root_second, [(32, 8, 512)], parts, second_weights), "ykx")
    parts, rows = call(
        pick_middle,
        [(32, 8, 128), (8, 8, 512)],
        parts,
        positions_middle.reshape(4, LANES),
        z_middle,
        coupling,
    )
    row = lax.dynamic_index_in_dim(rows, at(("y", "k")), 0, keepdims=False)
    solution_root = lax.dynamic_slice_in_dim(row, at(("a", "b", "d")) * 32, 32, 1)
    parts = exchange(parts, "ykx")
    middle_planes = call(hold, [(8, 64, QUARTER)], middle_planes)
    parts = exchange(call(middle_second, [(32, 8, 512)], parts, middle_planes), "ykx")
    parts, rows = call(
        pick_lower,
        [(4, 8, 128), (8, 8, 512)],
        parts,
        positions_lower.reshape(4, LANES),
        downward_lower,
    )
    row = lax.dynamic_index_in_dim(rows, at(("y", "k")), 0, keepdims=False)
    solution_middle = lax.dynamic_slice_in_dim(row, at(("b", "d")) * 64, 64, 1)
    parts = exchange(parts, "x")
    parts = exchange(call(subtract_spread, [(32, 8, 128)], parts, z_lower), "dyk")
    parts = exchange(call(lower_product, [(4, 8, 128)], parts, inverse_lower[1]), "x")
    solution_lower = call(sum_only, [(8, 128)], parts)
    return (solution_root, solution_middle, solution_lower)


def solution(mesh):
    split = Mesh(mesh.devices.reshape(tuple(SIZES.values())), tuple(SIZES))
    n = ("a", "b", "d", "y", "k")
    in_specs = (
        P(None, n),
        P(None, n),
        P(None, n),
        P(None, "x", n),
        P(None, "x", n),
        P(None, "x", n),
        P(n, "x"),
        P(n, "x"),
        P("x", n),
        P("x", n),
        P(None, "x"),
        P(None, "x"),
    )
    out_specs = (P(None, n), P(None, n), P(None, n))
    return jax.shard_map(local, mesh=split, in_specs=in_specs, out_specs=out_specs, check_vma=False)
```

```python
import jax
import jax.numpy as jnp
from jax import lax
from jax.experimental import pallas as pl
from jax.experimental.pallas import tpu as pltpu
from jax.sharding import Mesh
from jax.sharding import PartitionSpec as P

S = 4096
QUARTER = 1024
LANES = 128
SIZES = {"a": 2, "b": 2, "d": 4, "y": 4, "k": 2, "x": 4}
VMEM_LIMIT = 32 * 1024 * 1024


def count(axes):
    total = 1
    for axis in axes:
        total *= SIZES[axis]
    return total


def exchange(pieces, axes):
    return lax.all_to_all(pieces, tuple(axes), 0, 0, tiled=False)


def call(body, out_shapes, *operands, after=()):
    shapes = [jax.ShapeDtypeStruct(shape, jnp.float32) for shape in out_shapes]
    whole = pl.BlockSpec(memory_space=pltpu.VMEM)
    extra = len(after)
    return pl.pallas_call(
        lambda *refs: body(*refs[extra:]),
        out_shape=shapes[0] if len(shapes) == 1 else tuple(shapes),
        in_specs=[pl.BlockSpec(memory_space=pl.ANY)] * extra + [whole] * len(operands),
        out_specs=whole if len(shapes) == 1 else (whole,) * len(shapes),
        compiler_params=pltpu.CompilerParams(vmem_limit_bytes=VMEM_LIMIT),
    )(*after, *operands)


def product(left_side, right_side, transposed=False):
    def part(one, two):
        dims = (((1,), (1 if transposed else 0,)), ((), ()))
        return lax.dot_general(one, two, dims, preferred_element_type=jnp.float32)

    rows = left_side.shape[0]
    left_high = left_side.astype(jnp.bfloat16)
    left_low = (left_side - left_high.astype(jnp.float32)).astype(jnp.bfloat16)
    right_high = right_side.astype(jnp.bfloat16)
    right_low = (right_side - right_high.astype(jnp.float32)).astype(jnp.bfloat16)
    both = part(jnp.concatenate([left_high, left_low], axis=0), right_high)
    return both[:rows] + both[rows:] + part(left_high, right_low)


def spread(out_ref, value):
    for piece in range(out_ref.shape[0]):
        out_ref[piece] = value


def lane_ids():
    return lax.broadcasted_iota(jnp.int32, (8, LANES), 1)


def select_lanes(tiles, tile_at, lane_at):
    total = jnp.zeros((8, LANES), jnp.float32)
    for number, tile in enumerate(tiles):
        moved = jnp.take_along_axis(tile, lane_at, axis=1, mode="promise_in_bounds")
        total = jnp.where(tile_at == number, moved, total)
    return total


def row_of(index_ref, row):
    return jnp.broadcast_to(index_ref[row : row + 1, :], (8, LANES))


def sum_spread(parts_ref, out_ref):
    spread(out_ref, jnp.sum(parts_ref[...], axis=0))


def subtract_spread(parts_ref, kept_ref, out_ref):
    spread(out_ref, kept_ref[...] - jnp.sum(parts_ref[...], axis=0))


def sum_over_x(parts_ref):
    return [
        parts_ref[4 * i] + parts_ref[4 * i + 1] + parts_ref[4 * i + 2] + parts_ref[4 * i + 3]
        for i in range(8)
    ]


def regroup(sources):
    group = lane_ids() // 32
    total = jnp.zeros((8, LANES), jnp.float32)
    for to, (tile, start) in enumerate(sources):
        shift = ((to - start) * 32) % LANES
        moved = pltpu.roll(tile, shift, 1) if shift else tile
        total = jnp.where(group == to, moved, total)
    return total


def carve(planes_ref, first_ref, second_ref, coupling_ref):
    first_ref[...] = planes_ref[:, :32, :]
    second_ref[...] = planes_ref[:, 32:64, :]
    coupling_ref[...] = planes_ref[pl.ds(lax.axis_index("a") * 8, 8), 64:, :]


def hold(weights_ref, out_ref):
    out_ref[...] = weights_ref[...]


def stack_planes(root_ref, coupling_ref, planes_ref):
    planes_ref[:32] = root_ref[0]
    planes_ref[32:64] = root_ref[1]
    planes_ref[64:, :512] = coupling_ref[:32]
    planes_ref[64:, 512:] = coupling_ref[32:]


def spread_right(right_ref, out_ref):
    spread(out_ref, right_ref[...])


def map_sources(lower_ref, middle_ref, lower_out_ref, middle_out_ref):
    for index_ref, out_ref in ((lower_ref, lower_out_ref), (middle_ref, middle_out_ref)):
        index = jnp.concatenate([index_ref[i : i + 1, :] for i in range(4)], axis=1)
        number = lax.broadcasted_iota(jnp.int32, (32, 512), 1) + 1
        rows = jnp.broadcast_to(index >> 7, (32, 512)) == lax.broadcasted_iota(jnp.int32, (32, 512), 0)
        lanes = jnp.broadcast_to(index & 127, (LANES, 512)) == lax.broadcasted_iota(jnp.int32, (LANES, 512), 0)
        parts = [jnp.where(rows, part, 0).astype(jnp.float32) for part in (number >> 4, number & 15)]
        found = lax.dot_general(
            jnp.concatenate(parts, axis=0).astype(jnp.bfloat16),
            jnp.where(lanes, 1.0, 0.0).astype(jnp.bfloat16),
            (((1,), (1,)), ((), ())),
            preferred_element_type=jnp.float32,
        )
        out_ref[...] = found[:32] * 16.0 + found[32:] - 1.0


def hold_two(middle_ref, upward_ref, middle_out_ref, upward_out_ref):
    middle_out_ref[...] = middle_ref[1]
    upward_out_ref[...] = upward_ref[...]


def lower_last(parts_ref, weights_ref, out_ref):
    x_at = lax.axis_index("x")
    operand = jnp.concatenate([parts_ref[x_at * 8 + i] for i in range(8)], axis=1)
    out_ref[...] = product(operand, weights_ref[...])


def lower_product_first(parts_ref, weights_ref, middle_ref, upward_ref, source_ref, out_ref, copy_ref):
    copy_ref[...] = middle_ref[...]
    x_at = lax.axis_index("x")
    operand = jnp.concatenate([parts_ref[x_at * 8 + i] for i in range(8)], axis=1)
    value = product(operand, weights_ref[...])
    source = source_ref[...]
    for to in range(4):
        out_ref[to, :8] = value
        for tile in range(4):
            rows = slice(8 + 64 * tile, 8 + 64 * (tile + 1))
            out_ref[to, rows] = upward_ref[:, tile * LANES : (tile + 1) * LANES]
        out_ref[to, 264:] = source


def extend(tiles, sources, block_at, per_tile, right_ref, out_ref):
    for tile in range(32):
        source = jnp.broadcast_to(sources[tile : tile + 1], (8, LANES))
        out_ref[(tile % 8) * 4 + tile // 8] = -select_lanes(tiles, source >> 7, source & 127)
    tile_at = block_at // per_tile
    piece_at = (tile_at % 8) * 4 + tile_at // 8
    out_ref[piece_at] = out_ref[piece_at] + right_ref[...]


def lower_extend(parts_ref, weights_ref, source_ref, right_ref, out_ref, kept_ref):
    value = jnp.sum(parts_ref[:, :8, :], axis=0)
    kept_ref[...] = value
    update = product(value, weights_ref[...])
    tiles = [update[:, i * LANES : (i + 1) * LANES] for i in range(4)]
    extend(tiles, source_ref[...].astype(jnp.int32), lax.axis_index(("b", "d", "y", "k")), 2, right_ref, out_ref)


def middle_extend(parts_ref, weights_ref, moved_ref, right_ref, out_ref, kept_ref):
    operand = jnp.concatenate([parts_ref[i] for i in range(8)], axis=1)
    doubled = jnp.concatenate([weights_ref[...], weights_ref[...]], axis=0)
    value = product(operand, doubled, True)
    kept_ref[...] = value
    tiles = []
    sources = jnp.full((32, LANES), -1.0, jnp.float32)
    for x in range(4):
        upward = [moved_ref[x, 8 + 64 * tile : 8 + 64 * (tile + 1), :] for tile in range(4)]
        update = product(value[:, :64], jnp.concatenate(upward, axis=1))
        tiles += [update[:, i * LANES : (i + 1) * LANES] for i in range(4)]
        number = moved_ref[x, 264:, :]
        sources = jnp.maximum(sources, jnp.where(number >= 0, number + 512.0 * x, -1.0))
    sources = sources.astype(jnp.int32)
    extend(tiles, sources, lax.axis_index(("a", "b", "d", "y", "k")), 4, right_ref, out_ref)


def stack_spread(parts_ref, kept_ref, out_ref):
    value = jnp.sum(parts_ref[...], axis=0)
    for piece in range(16):
        out_ref[piece, :8] = value
        out_ref[piece, 8:] = kept_ref[...]


def unstack_spread(parts_ref, out_ref, kept_ref):
    spread(out_ref, jnp.sum(parts_ref[:, :8, :], axis=0))
    first = lax.axis_index("a") * 8
    for tile in range(2):
        blocks = [parts_ref[first + tile * 4 + i, 8:, :] for i in range(4)]
        for half in range(2):
            kept_ref[half * 2 + tile] = regroup([(block, half) for block in blocks])


def root_first(parts_ref, weights_ref, out_ref):
    operand = jnp.concatenate([parts_ref[i] for i in range(8)], axis=1)
    for step in range(4):
        weights = weights_ref[step * 4 : step * 4 + 4].reshape(LANES, QUARTER)
        value = product(operand, weights, True)
        for row in range(8):
            out_ref[row * 4 + step] = value


def spread_product(out_ref, operand, weights_at):
    for step in range(4):
        value = product(operand, weights_at(step).reshape(LANES, QUARTER), True)
        for piece in range(out_ref.shape[0]):
            out_ref[piece, :, step * LANES : (step + 1) * LANES] = value


def root_second(parts_ref, weights_ref, out_ref):
    rows = sum_over_x(parts_ref)
    tiles = [regroup([(rows[(i % 2) * 4 + t], i // 2) for t in range(4)]) for i in range(8)]
    operand = jnp.concatenate(tiles, axis=1)
    spread_product(out_ref, operand, lambda step: weights_ref[step * 4 : step * 4 + 4])


def pick_middle(parts_ref, index_ref, kept_ref, weights_ref, out_ref, rows_ref):
    rows = sum_over_x(parts_ref)
    for i in range(8):
        rows_ref[i] = rows[i]
    tiles = [rows[i // 4][:, (i % 4) * LANES : (i % 4 + 1) * LANES] for i in range(32)]
    picked = []
    for i in range(4):
        at = row_of(index_ref, i)
        plane = at >> 8
        tile_at = ((at >> 5) & 7) * 4 + (plane >> 2)
        picked.append(select_lanes(tiles, tile_at, (plane & 3) * 32 + (at & 31)))
    operand = jnp.concatenate(picked, axis=1)
    values = []
    for half in range(2):
        weights = weights_ref[:, :, half * 512 : (half + 1) * 512].reshape(256, 512)
        coupled = product(operand, weights, True)
        for tile in range(2):
            values.append(kept_ref[half * 2 + tile] - coupled[:, tile * LANES : (tile + 1) * LANES])
    for to in range(4):
        low, high = values[to // 2], values[2 + to // 2]
        start = (to % 2) * 2
        value = regroup([(low, start), (low, start + 1), (high, start), (high, start + 1)])
        for row in range(8):
            out_ref[row * 4 + to] = value


def middle_second(parts_ref, weights_ref, out_ref):
    rows = sum_over_x(parts_ref)
    tiles = []
    for i in range(8):
        pair = [rows[(i % 4) * 2], rows[(i % 4) * 2 + 1]]
        tiles.append(regroup([(pair[g // 2], (g % 2) * 2 + i // 4) for g in range(4)]))
    operand = jnp.concatenate(tiles, axis=1)
    spread_product(out_ref, operand, lambda step: weights_ref[step * 2 : step * 2 + 2])


def pick_lower(parts_ref, index_ref, weights_ref, out_ref, rows_ref):
    rows = sum_over_x(parts_ref)
    for i in range(8):
        rows_ref[i] = rows[i]
    tiles = [rows[i // 4][:, (i % 4) * LANES : (i % 4 + 1) * LANES] for i in range(32)]
    picked = []
    for i in range(4):
        at = row_of(index_ref, i)
        tile_at = ((at >> 6) & 7) * 4 + (at >> 10)
        picked.append(select_lanes(tiles, tile_at, ((at >> 9) & 1) * 64 + (at & 63)))
    spread(out_ref, product(jnp.concatenate(picked, axis=1), weights_ref[...]))


def placed(right_block, at):
    width = right_block.shape[1]
    times = LANES // width
    lanes = jnp.arange(LANES, dtype=jnp.int32)[None, :] // width
    here = (lanes == at % times) & (lax.axis_index("x") == 0)
    return jnp.where(here, jnp.tile(right_block, (1, times)), 0.0)


def local(
    right_root,
    right_middle,
    right_lower,
    inverse_root,
    inverse_middle,
    inverse_lower,
    upward_middle,
    upward_lower,
    downward_middle,
    downward_lower,
    index_middle,
    index_lower,
):
    at = lax.axis_index
    n = ("a", "b", "d", "y", "k")
    positions_middle = lax.dynamic_index_in_dim(index_middle, at("a"), 0, keepdims=False)
    positions_lower = lax.dynamic_index_in_dim(index_lower, at(("a", "b")), 0, keepdims=False)
    right_middle_tile = placed(right_middle, at(("b", "d", "y", "k")))
    right_root_tile = placed(right_root, at(n))
    source_lower, source_middle = call(
        map_sources,
        [(32, LANES), (32, LANES)],
        positions_lower.reshape(4, LANES),
        positions_middle.reshape(4, LANES),
    )

    planes = call(stack_planes, [(96, QUARTER)], inverse_root.transpose(0, 2, 1), downward_middle.T)
    parts = call(spread_right, [(32, 8, 128)], right_lower, after=(planes,))
    planes = lax.all_gather(planes, ("a", "b", "d"), axis=0)

    parts = exchange(parts, "dyk")
    middle_own, upward_own = call(
        hold_two,
        [(64, QUARTER), (64, 512)],
        inverse_middle.transpose(0, 2, 1),
        upward_middle,
        after=(source_lower,),
    )
    moved, middle_planes = call(
        lower_product_first,
        [(4, 296, 128), (64, QUARTER)],
        parts,
        inverse_lower[0],
        middle_own,
        upward_own,
        source_middle,
        after=(source_lower, right_middle_tile),
    )
    middle_planes = lax.all_gather(middle_planes, ("b", "d"), axis=0)
    moved = exchange(moved, "x")
    parts, z_lower = call(
        lower_extend, [(32, 8, 128), (8, 128)], moved, upward_lower, source_lower, right_middle_tile
    )
    parts = exchange(parts, "ykx")
    parts = exchange(call(sum_spread, [(8, 8, 128)], parts), "bd")
    parts = exchange(call(sum_spread, [(8, 8, 128)], parts), "yk")
    parts, z_middle = call(
        middle_extend,
        [(32, 8, 128), (8, 128)],
        parts,
        inverse_middle[0].T,
        moved,
        right_root_tile,
    )
    parts = exchange(parts, "ykx")
    parts = exchange(call(stack_spread, [(16, 16, 128)], parts, z_middle), "abd")
    first_weights, second_weights, coupling = call(
        carve, [(16, 32, QUARTER), (16, 32, QUARTER), (8, 32, QUARTER)], planes
    )
    parts, z_middle = call(unstack_spread, [(8, 8, 128), (4, 8, 128)], parts, after=(first_weights,))
    parts = exchange(parts, "yk")
    parts = exchange(call(root_first, [(32, 8, 128)], parts, first_weights), "ykx")
    parts = exchange(call(root_second, [(32, 8, 512)], parts, second_weights), "ykx")
    parts, rows = call(
        pick_middle,
        [(32, 8, 128), (8, 8, 512)],
        parts,
        positions_middle.reshape(4, LANES),
        z_middle,
        coupling,
    )
    row = lax.dynamic_index_in_dim(rows, at(("y", "k")), 0, keepdims=False)
    solution_root = lax.dynamic_slice_in_dim(row, at(("a", "b", "d")) * 32, 32, 1)
    parts = exchange(parts, "ykx")
    middle_planes = call(hold, [(8, 64, QUARTER)], middle_planes)
    parts = exchange(call(middle_second, [(32, 8, 512)], parts, middle_planes), "ykx")
    parts, rows = call(
        pick_lower,
        [(4, 8, 128), (8, 8, 512)],
        parts,
        positions_lower.reshape(4, LANES),
        downward_lower,
    )
    row = lax.dynamic_index_in_dim(rows, at(("y", "k")), 0, keepdims=False)
    solution_middle = lax.dynamic_slice_in_dim(row, at(("b", "d")) * 64, 64, 1)
    parts = exchange(parts, "x")
    parts = exchange(call(subtract_spread, [(32, 8, 128)], parts, z_lower), "dyk")
    solution_lower = lax.psum(call(lower_last, [(8, 128)], parts, inverse_lower[1]), "x")
    return (solution_root, solution_middle, solution_lower)


def solution(mesh):
    split = Mesh(mesh.devices.reshape(tuple(SIZES.values())), tuple(SIZES))
    n = ("a", "b", "d", "y", "k")
    in_specs = (
        P(None, n),
        P(None, n),
        P(None, n),
        P(None, "x", n),
        P(None, "x", n),
        P(None, "x", n),
        P(n, "x"),
        P(n, "x"),
        P("x", n),
        P("x", n),
        P(None, "x"),
        P(None, "x"),
    )
    out_specs = (P(None, n), P(None, n), P(None, n))
    return jax.shard_map(local, mesh=split, in_specs=in_specs, out_specs=out_specs, check_vma=False)
```
